256 devices in a mesh: grp: 16 (over y, z_lo), tp: 16 (over x, z_hi, core).
Axes of the slice: x: 4, y: 4, z: 8 (z_hi: 2, z_lo: 4; z = z_hi * 4 + z_lo), core: 2. Of those that a mesh axis runs over, the one named last changes fastest.
Arguments:
- teacher_rows: bfloat16 [32768, 8192], P(('grp', 'tp')), may hold values from -6 to 6
- student_rows: bfloat16 [32768, 2048], P(('grp', 'tp')), may hold values from -24 to 24
- proj: bfloat16 [2048, 8192], P(None, 'tp'), may hold values from -0.125 to 0.125
Outputs:
- grad_proj: float32 [2048, 8192], P('grp', 'tp')
- grad_student: bfloat16 [32768, 2048], P(('grp', 'tp'))
The draws below stay inside these ranges and needn't reach their ends.
All inputs are finite; a program needn't handle non-finite values.
Results may differ from the reference program's by a relative error of at most 0.019.
Values may be sent and summed in bfloat16 or wider, within the bound.
No kernel may reach another device: no remote copies, remote signals or barrier semaphores. Data moves between devices by JAX's collectives and lax.ppermute only.
A program may use at most 192 MiB of HBM per device.

```python
import math
import jax
import jax.numpy as jnp
from jax import lax

DS = 2048
DT = 8192
TOKENS = 32768
N_TP = 16


def strengthened(array, key, source, target, parts, factor):
    owner, partner = [(jnp.arange(array.shape[position]) // (array.shape[position] // parts)).reshape([-1 if axis == position else 1 for axis in range(array.ndim)]) for position in (source, target)]
    chosen = jax.random.permutation(key, parts)[partner]
    strong = (owner == chosen) | (owner == (partner + parts // 2) % parts)
    return jnp.where(strong, factor * array, array)


def level_of(own_key, extent, pieces, smallest, top_value):
    loudness, own = 1.0, jax.random.fold_in(own_key, 6)
    for axis_at, shards_of in pieces:
        draws = jnp.exp(jax.random.uniform(jax.random.fold_in(own, axis_at), (shards_of,), jnp.float32, smallest / len(pieces), top_value / len(pieces)))
        loudness = loudness * jnp.repeat(draws, extent[axis_at] // shards_of).reshape([-1 if axis == axis_at else 1 for axis in range(len(extent))])
    return loudness


def scatter_about(rng, dims, spread, limit, cuts=(), held_as=jnp.bfloat16):
    drawn = jax.random.normal(rng, dims, jnp.float32) * spread
    if len(cuts) > 0:
        drawn = level_of(rng, dims, cuts, -0.22, 0.18) * drawn
    return jnp.clip(drawn, min=-limit, max=limit).astype(held_as)


def heavy_noise(stream_key, shape, width, bound, split, heavy, held_as=jnp.bfloat16):
    array = width * jax.random.normal(stream_key, shape, jnp.float32)
    if split:
        array = array * level_of(stream_key, shape, split, -0.22, 0.18)
    return jnp.clip(strengthened(array, jax.random.fold_in(stream_key, 3), *heavy), -bound, bound).astype(held_as)


def setup_inputs(seed: int = 0) -> dict:
    seeds = jax.random.split(jax.random.key(seed), 4)
    teacher_rows = scatter_about(seeds[0], (TOKENS, DT), 1.0, 6.0, ((0, 256),))
    student_rows = heavy_noise(seeds[1], (TOKENS, DS), 1.0, 24.0, ((0, 256),), (0, 1, 256, 6.0))
    proj = scatter_about(seeds[2], (DS, DT), DS ** -0.5, 0.125, ((1, 16),))
    return {"teacher_rows": teacher_rows, "student_rows": student_rows, "proj": proj}


def grouped_sum(left_groups, right_groups, rows, cols):

    def add_group(carry, pair):
        term = jnp.dot(pair[0], pair[1], preferred_element_type=jnp.float32)
        rounded = lax.optimization_barrier(term.astype(jnp.bfloat16))
        return (carry + rounded.astype(jnp.float32), None)
    summed, _ = lax.scan(add_group, jnp.zeros((rows, cols), jnp.float32), (left_groups, right_groups))
    return summed

def reference(teacher_rows, student_rows, proj):
    predicted = jnp.dot(student_rows, proj, preferred_element_type=jnp.float32)
    error = (predicted - teacher_rows.astype(jnp.float32)).astype(jnp.bfloat16)
    factor = 1.0 / math.sqrt(TOKENS)
    grad_proj = jnp.dot(student_rows.T, error, preferred_element_type=jnp.float32) * factor
    col_width = DT // N_TP
    error_groups = error.reshape(TOKENS, N_TP, col_width).transpose(1, 0, 2)
    proj_groups = proj.reshape(DS, N_TP, col_width).transpose(1, 2, 0)
    grad_student = grouped_sum(error_groups, proj_groups, TOKENS, DS).astype(jnp.bfloat16)
    return (grad_proj, grad_student)
```

```python
import math

import jax
import jax.numpy as jnp
from jax import lax
from jax.sharding import Mesh
from jax.sharding import PartitionSpec as P

F32 = jnp.float32
BF16 = jnp.bfloat16
ALL = ("y", "zl", "x", "zh", "c")
Z_AXES = ("zl", "zh")


def shift(array, axis, by):
    n = lax.axis_size(axis)
    return lax.ppermute(array, axis, [(i, (i + by) % n) for i in range(n)])


def shift_z(array, by_lo):
    pairs = [
        (lo * 2 + hi, ((lo + by_lo) % 4) * 2 + 1 - hi) for lo in range(4) for hi in range(2)
    ]
    return lax.ppermute(array, Z_AXES, pairs)


def matmul(a, b, da, db):
    return lax.dot_general(a, b, (((da,), (db,)), ((), ())), preferred_element_type=F32)


def body(teacher, student, proj):
    y, zl, x, zh, c = (lax.axis_index(a) for a in ALL)
    tok, ds = student.shape
    width = proj.shape[1]
    n_x, n_y, n_zl = 4, 4, 4
    factor = 1.0 / math.sqrt(tok * 256)

    def piece(x_at, zh_at, c_at):
        start = ((x_at * 2 + zh_at) * 2 + c_at) * width
        return lax.dynamic_slice(teacher, (0, start), (tok, width))

    def pair(x_at, zh_at):
        return jnp.concatenate([piece(x_at, zh_at, c), piece(x_at, zh_at, 1 - c)], axis=1)

    rows = ds // (n_y * n_zl)
    part = lax.dynamic_slice(proj, ((y * n_zl + zl) * rows, 0), (rows, width))
    proj_c = lax.all_gather(shift(part, "zh", 1), ("y", "zl"), axis=0, tiled=True)
    proj_b = shift(proj, "c", 1)
    proj_d = shift(proj_c, "c", 1)

    students = jnp.concatenate([student] + [shift(student, "x", s) for s in (1, 2, 3)], axis=0)
    halves = []
    for zh_at in (zh, 1 - zh):
        blocks = [pair(x, zh_at)]
        blocks += [shift(pair((x + s) % n_x, zh_at), "x", s) for s in (1, 2, 3)]
        halves.append(jnp.concatenate(blocks, axis=0))

    def error(weights, target):
        return (matmul(students, weights, 1, 0) - target.astype(F32)).astype(BF16)

    pieces = [
        (proj, halves[0][:, :width]),
        (proj_b, halves[0][:, width:]),
        (proj_c, halves[1][:, :width]),
        (proj_d, halves[1][:, width:]),
    ]
    errors = [error(w, t) for w, t in pieces]

    def reduced_over_y(own, other):
        received = shift(matmul(students, other, 0, 0).astype(BF16), "c", 1)
        both = (matmul(students, own, 0, 0) + received.astype(F32)).astype(BF16)
        block = ds // n_y

        def rows_of(y_at):
            return lax.dynamic_slice(both, (y_at * block, 0), (block, width))

        total = rows_of(y).astype(F32)
        for s in (1, 2, 3):
            total = total + shift(rows_of((y + s) % n_y), "y", s).astype(F32)
        return total

    def rows_for(array, zl_at):
        return lax.dynamic_slice(array, (zl_at * rows, 0), (rows, width))

    near = reduced_over_y(errors[0], errors[1])
    near16 = near.astype(BF16)
    grad_proj = rows_for(near, zl)
    for s in (1, 2, 3):
        grad_proj = grad_proj + shift(rows_for(near16, (zl + s) % n_zl), "zl", s).astype(F32)
    far = reduced_over_y(errors[2], errors[3]).astype(BF16)
    for s in range(4):
        grad_proj = grad_proj + shift_z(rows_for(far, (zl + s) % n_zl), s).astype(F32)
    grad_proj = grad_proj * factor

    partial = matmul(
        jnp.concatenate(errors, axis=1),
        jnp.concatenate([w for w, _ in pieces], axis=1),
        1,
        1,
    ).astype(BF16)
    total = partial[:tok].astype(F32)
    for s in (1, 2, 3):
        total = total + shift(partial[s * tok : (s + 1) * tok], "x", -s).astype(F32)
    return grad_proj, total.astype(BF16)


def solution(mesh):
    fine = Mesh(mesh.devices.reshape(4, 4, 4, 2, 2), ALL)
    tokens = P(ALL, None)
    return jax.shard_map(
        body,
        mesh=fine,
        in_specs=(tokens, tokens, P(None, ("x", "zh", "c"))),
        out_specs=(P(("y", "zl"), ("x", "zh", "c")), tokens),
        check_vma=False,
    )
```

```python
import functools
import math

import jax
import jax.numpy as jnp
from jax import lax
from jax.experimental import pallas as pl
from jax.experimental.pallas import tpu as pltpu
from jax.sharding import Mesh
from jax.sharding import PartitionSpec as P

F32 = jnp.float32
BF16 = jnp.bfloat16
ALL = ("y", "zl", "x", "zh", "c")
ANY = pl.BlockSpec(memory_space=pl.ANY)
VMEM = pl.BlockSpec(memory_space=pltpu.VMEM)
N = 4
TOK, DS, WIDTH = 128, 2048, 512
BLOCK = DS // N
ROWS = BLOCK // N
BIG = 10**11


def shift(array, axis, by):
    n = lax.axis_size(axis)
    return lax.ppermute(array, axis, [(i, (i + by) % n) for i in range(n)])


def after(value, *done):
    return lax.optimization_barrier((value, *done))[0]


def index(axis):
    return lax.axis_index(axis)


def columns(x_at, zh_at, c_at):
    return pl.ds(pl.multiple_of(((x_at * 2 + zh_at) * 2 + c_at) * WIDTH, WIDTH), WIDTH)


def place(at, size):
    return pl.ds(pl.multiple_of(at * size, size), size)


def pieces(zh, c):
    return ((zh, c), (zh, 1 - c), (1 - zh, c), (1 - zh, 1 - c))


def dot(a, b, da, db):
    return lax.dot_general(a, b, (((da,), (db,)), ((), ())), preferred_element_type=F32)


def call(kernel, ins, out_shapes, scratch, mib, flops=1, out_specs=None, in_specs=None):
    return pl.pallas_call(
        kernel,
        in_specs=in_specs or [ANY] * len(ins),
        out_specs=out_specs or [ANY] * len(out_shapes),
        out_shape=[jax.ShapeDtypeStruct(s, t) for s, t in out_shapes],
        scratch_shapes=scratch,
        cost_estimate=pl.CostEstimate(flops=flops, bytes_accessed=1, transcendentals=0),
        compiler_params=pltpu.CompilerParams(vmem_limit_bytes=mib * 2**20),
    )(*ins)


def run(pairs, sems, first=0):
    copies = [
        pltpu.make_async_copy(src, dst, sems.at[first + i]) for i, (src, dst) in enumerate(pairs)
    ]
    for copy in copies:
        copy.start()
    return copies


def cut_kernel(proj, part, sem):
    copy = pltpu.make_async_copy(proj.at[place(index("y"), BLOCK), :], part, sem)
    copy.start()
    copy.wait()


def cut(proj):
    return call(
        cut_kernel,
        (proj,),
        [((BLOCK, WIDTH), BF16)],
        [pltpu.SemaphoreType.DMA],
        4,
        out_specs=[VMEM],
    )[0]


def split_kernel(teacher, o1, o3, o2, sems):
    x, zh, c = (index(a) for a in ("x", "zh", "c"))
    pairs = []
    for s, out in ((1, o1), (3, o3), (2, o2)):
        for j, (zh_at, c_at) in enumerate(pieces(zh, c)):
            pairs.append(
                (
                    teacher.at[:, columns((x + s) % N, zh_at, c_at)],
                    out.at[:, pl.ds(j * WIDTH, WIDTH)],
                )
            )
    for copy in run(pairs, sems):
        copy.wait()


def split(teacher):
    return call(
        split_kernel,
        (teacher,),
        [((TOK, 4 * WIDTH), BF16)] * 3,
        [pltpu.SemaphoreType.DMA((12,))],
        8,
        BIG,
        out_specs=[VMEM] * 3,
    )


def join_kernel(own, p1, p2, p3, out, sems):
    y = index("y")
    pairs = [
        (ref, out.at[place((y + N - s) % N, BLOCK), :]) for s, ref in enumerate((own, p1, p2, p3))
    ]
    for copy in run(pairs, sems):
        copy.wait()


def join(parts):
    return call(
        join_kernel,
        parts,
        [((DS, WIDTH), BF16)],
        [pltpu.SemaphoreType.DMA((4,))],
        8,
        out_specs=[VMEM],
    )[0]


def error_kernel(half, s0, s1, s2, s3, w_own, w_other, teacher, t1, t2, t3, *rest):
    error, grad, students, weights, targets, errors, grads, sems, out_sems = rest
    x, zh, c = (index(a) for a in ("x", "zh", "c"))
    zh_at = zh if half == 0 else 1 - zh
    spots = [place((x + N - s) % N, TOK) for s in range(N)]
    first = run(
        [(ref, students.at[spot, :]) for ref, spot in zip((s0, s1, s2, s3), spots)]
        + [(w_other, weights.at[1])],
        sems,
    )
    second = run(
        [
            (ref.at[:, pl.ds(half * 2 * WIDTH, 2 * WIDTH)], targets.at[spot, :])
            for ref, spot in zip((t1, t2, t3), spots[1:])
        ]
        + [
            (
                teacher.at[:, columns(x, zh_at, c_at)],
                targets.at[spots[0], pl.ds(j * WIDTH, WIDTH)],
            )
            for j, c_at in enumerate((c, 1 - c))
        ]
        + [(w_own, weights.at[0])],
        sems,
        5,
    )
    for copy in first + second[:-1]:
        copy.wait()

    def one(j):
        for n in range(2):
            cols = pl.ds(j * WIDTH + n * 256, 256)
            predicted = dot(students[...], weights[j, :, pl.ds(n * 256, 256)], 1, 0)
            errors[:, cols] = (predicted - targets[:, cols].astype(F32)).astype(BF16)

    one(1)
    turned = errors[:, pl.ds(WIDTH, WIDTH)].T
    for n in range(N):
        cols = pl.ds(n * BLOCK, BLOCK)
        grads[:, cols] = dot(turned, students[:, cols], 1, 0).astype(BF16)
    out = run([(grads, grad)], out_sems)
    second[-1].wait()
    one(0)
    out += run([(errors, error)], out_sems, 1)
    for copy in out:
        copy.wait()


def error_and_other(half, students, w_own, w_other, teacher, targets):
    n_tok = N * TOK
    return call(
        functools.partial(error_kernel, half),
        (*students, w_own, w_other, teacher, *targets),
        [((n_tok, 2 * WIDTH), BF16), ((WIDTH, DS), BF16)],
        [
            pltpu.VMEM((n_tok, DS), BF16),
            pltpu.VMEM((2, DS, WIDTH), BF16),
            pltpu.VMEM((n_tok, 2 * WIDTH), BF16),
            pltpu.VMEM((n_tok, 2 * WIDTH), BF16),
            pltpu.VMEM((WIDTH, DS), BF16),
            pltpu.SemaphoreType.DMA((11,)),
            pltpu.SemaphoreType.DMA((2,)),
        ],
    18,
        BIG,
    )


def own_kernel(order, s0, s1, s2, s3, error, there, *rest):
    ins, rest = rest[: len(order) - 1], rest[len(order) - 1 :]
    outs, rest = rest[: 2 if order == (2,) else 3], rest[2 if order == (2,) else 3 :]
    students, errors, theirs, passed, grads, sems, there_sems, out_sems = rest
    x, y = index("x"), index("y")
    spots = [place((x + N - s) % N, TOK) for s in range(N)]
    begun = run([(error.at[:, pl.ds(0, WIDTH)], errors)], sems)
    begun += run([(ref, passed.at[i]) for i, ref in enumerate(ins)], sems, 13)
    loads = []
    for k, s in enumerate(order):
        cols = place((y + s) % N, BLOCK)
        loads.append(
            run(
                [
                    (ref.at[:, cols], students.at[k, spot, :])
                    for ref, spot in zip((s0, s1, s2, s3), spots)
                ],
                sems,
                1 + 4 * k,
            )
            + run([(there.at[:, cols], theirs.at[k])], there_sems, k)
        )
    for copy in begun:
        copy.wait()
    turned = errors[...].T
    out = []
    half = WIDTH // 2
    for k, s in enumerate(order):
        for copy in loads[k]:
            copy.wait()
        total = dot(turned, students[k], 1, 0) + theirs[k].astype(F32)
        if s == 1:
            grads[k, :half] = (total[:half] + passed[0].astype(F32)).astype(BF16)
            grads[k, half:] = total[half:].astype(BF16)
        elif s == 3:
            grads[k, :half] = total[:half].astype(BF16)
            grads[k, half:] = (total[half:] + passed[1].astype(F32)).astype(BF16)
        else:
            grads[k] = total.astype(BF16)
        if s == 2:
            out += run(
                [(grads.at[k, :half], outs[0]), (grads.at[k, half:], outs[1])], out_sems
            )
        else:
            out += run([(grads.at[k], outs[k])], out_sems, k)
    for copy in out:
        copy.wait()


def own_and_sum(order, students, error, there, ins=()):
    n_tok, n = N * TOK, len(order)
    halves = [((WIDTH // 2, BLOCK), BF16)] * 2
    return call(
        functools.partial(own_kernel, order),
        (*students, error, there, *ins),
        halves if order == (2,) else [((WIDTH, BLOCK), BF16)] * 3,
        [
            pltpu.VMEM((n, n_tok, BLOCK), BF16),
            pltpu.VMEM((n_tok, WIDTH), BF16),
            pltpu.VMEM((n, WIDTH, BLOCK), BF16),
            pltpu.VMEM((2, WIDTH // 2, BLOCK), BF16),
            pltpu.VMEM((n, WIDTH, BLOCK), BF16),
            pltpu.SemaphoreType.DMA((15,)),
            pltpu.SemaphoreType.DMA((3,)),
            pltpu.SemaphoreType.DMA((3,)),
        ],
        12,
    )


def student_kernel(near, far, wa, wb, wc, wd, o0, o1, o3, o2, *rest):
    errors, weights, grads, sems, out_sems = rest
    x = index("x")
    loads = run([(near, errors.at[0]), (far, errors.at[1])], sems)
    loads += run([(w, weights.at[i]) for i, w in enumerate((wa, wb, wc, wd))], sems, 2)
    for copy in loads:
        copy.wait()
    stores = []
    for n in range(N):
        cols = pl.ds(n * BLOCK, BLOCK)
        total = None
        for p in range(4):
            term = dot(errors[p // 2, :, pl.ds(p % 2 * WIDTH, WIDTH)], weights[p, cols, :], 1, 1)
            total = term if total is None else total + term
        grads[:, cols] = total.astype(BF16)
        stores += run(
            [
                (grads.at[place((x + s) % N, TOK), cols], out.at[:, cols])
                for s, out in enumerate((o0, o1, o2, o3))
            ],
            out_sems,
            4 * n,
        )
    for copy in stores:
        copy.wait()


def student_part(near, far, weights):
    n_tok = N * TOK
    return call(
        student_kernel,
        (near, far, *weights),
        [((TOK, DS), BF16)] * 4,
        [
            pltpu.VMEM((2, n_tok, 2 * WIDTH), BF16),
            pltpu.VMEM((4, DS, WIDTH), BF16),
            pltpu.VMEM((n_tok, DS), BF16),
            pltpu.SemaphoreType.DMA((6,)),
            pltpu.SemaphoreType.DMA((16,)),
        ],
        20,
        BIG,
    )


def y_kernel(a, b, c, *outs):
    zl = index("zl")
    for s, out in zip((0, 1, 3, 2), outs):
        cols = place((zl + s) % N, ROWS)
        total = a[:, cols].astype(F32) + b[:, cols].astype(F32) + c[:, cols].astype(F32)
        out[...] = total.astype(out.dtype)


def z_kernel(own, p1, p2, p3, out):
    total = own[...] + p1[...].astype(F32) + p2[...].astype(F32) + p3[...].astype(F32)
    out[...] = total.astype(BF16)


def final_kernel(own, p1, p2, p3, far, out):
    total = own[...] + p1[...].astype(F32) + p2[...].astype(F32) + p3[...].astype(F32)
    out[...] = (total + far[...].astype(F32)).T * (1.0 / math.sqrt(TOK * 256))


def student_sum_kernel(own, p1, p2, p3, out):
    total = own[...].astype(F32) + p1[...].astype(F32)
    out[...] = (total + p2[...].astype(F32) + p3[...].astype(F32)).astype(BF16)


def in_vmem(kernel, ins, outs):
    return call(kernel, ins, outs, [], 8, in_specs=[VMEM] * len(ins), out_specs=[VMEM] * len(outs))


def over(axis, blocks, *done):
    got = {s: shift(after(b, *done), axis, s) for s, b in zip((1, 3, 2), blocks)}
    return [got[s] for s in (1, 2, 3)]


def body(teacher, student, proj):
    students = [student] + over("x", [student] * 3)
    part = shift(cut(proj), "zh", 1)
    proj_b = shift(proj, "c", 1)
    sends = split(after(teacher, *students[1:]))
    targets = over("x", sends)

    proj_c = join([part, *over("y", [part] * 3)])
    proj_d = shift(proj_c, "c", 1)

    near, near_other = error_and_other(0, students, after(proj, proj_c), proj_b, teacher, targets)
    near_there = shift(near_other, "c", 1)
    far, far_other = error_and_other(1, students, after(proj_c, near), proj_d, teacher, targets)
    far_there = shift(far_other, "c", 1)

    blocks = own_and_sum((2,), students, near, after(near_there, far))
    near_in = [shift(blocks[0], "y", 1), shift(blocks[1], "y", 3)]
    partial = student_part(near, far, (proj, proj_b, proj_c, after(proj_d, *blocks)))
    blocks = own_and_sum((1, 3, 0), students, near, after(near_there, partial[0]), near_in)
    near_y = [blocks[2], shift(blocks[0], "y", 1), shift(blocks[1], "y", 3)]
    blocks = own_and_sum((2,), students, far, after(far_there, *blocks))
    far_in = [shift(blocks[0], "y", 1), shift(blocks[1], "y", 3)]
    back2 = shift(after(partial[3], *blocks), "x", 2)
    blocks = own_and_sum((1, 3, 0), students, far, far_there, far_in)

    def over_y(terms):
        return in_vmem(
            y_kernel, terms, [((WIDTH, ROWS), F32)] + [((WIDTH, ROWS), BF16)] * 3
        )

    near_z = over_y(near_y)
    ready = after(blocks[0], *near_z), after(blocks[1], *near_z)
    far_y = [blocks[2], shift(ready[0], "y", 1), shift(ready[1], "y", 3)]
    near_terms = [near_z[0]] + over("zl", near_z[1:])
    back1 = shift(after(partial[1], *blocks), "x", 1)
    back3 = shift(after(partial[2], *blocks), "x", 3)
    far_z = over_y([after(far_y[0], back1, back2, back3, *near_terms), *far_y[1:]])
    far_terms = [far_z[0]] + over("zl", far_z[1:])
    far_part = in_vmem(z_kernel, far_terms, [((WIDTH, ROWS), BF16)])[0]
    far_part = shift(far_part, "zh", 1)
    grad_student = in_vmem(
        student_sum_kernel, [partial[0], back1, back2, back3], [((TOK, DS), BF16)]
    )[0]
    grad_proj = in_vmem(final_kernel, [*near_terms, far_part], [((ROWS, WIDTH), F32)])[0]
    return grad_proj, grad_student


def solution(mesh):
    fine = Mesh(mesh.devices.reshape(4, 4, 4, 2, 2), ALL)
    tokens = P(ALL, None)
    return jax.shard_map(
        body,
        mesh=fine,
        in_specs=(tokens, tokens, P(None, ("x", "zh", "c"))),
        out_specs=(P(("y", "zl"), ("x", "zh", "c")), tokens),
        check_vma=False,
    )
```

```python
import functools
import math

import jax
import jax.numpy as jnp
from jax import lax
from jax.experimental import pallas as pl
from jax.experimental.pallas import tpu as pltpu
from jax.sharding import Mesh
from jax.sharding import PartitionSpec as P

F32 = jnp.float32
BF16 = jnp.bfloat16
ALL = ("y", "zl", "x", "zh", "c")
ANY = pl.BlockSpec(memory_space=pl.ANY)
VMEM = pl.BlockSpec(memory_space=pltpu.VMEM)
N = 4
TOK, DS, WIDTH = 128, 2048, 512
BLOCK = DS // N
ROWS = BLOCK // N
BIG = 10**11
SMALL = 3 * 10**8


def shift(array, axis, by):
    n = lax.axis_size(axis)
    return lax.ppermute(array, axis, [(i, (i + by) % n) for i in range(n)])


def after(value, *done):
    return lax.optimization_barrier((value, *done))[0]


def index(axis):
    return lax.axis_index(axis)


def columns(x_at, zh_at, c_at):
    return pl.ds(pl.multiple_of(((x_at * 2 + zh_at) * 2 + c_at) * WIDTH, WIDTH), WIDTH)


def place(at, size):
    return pl.ds(pl.multiple_of(at * size, size), size)


def pieces(zh, c):
    return ((zh, c), (zh, 1 - c), (1 - zh, c), (1 - zh, 1 - c))


def dot(a, b, da, db):
    return lax.dot_general(a, b, (((da,), (db,)), ((), ())), preferred_element_type=F32)


def call(kernel, ins, out_shapes, scratch, mib, flops=1, out_specs=None, in_specs=None):
    return pl.pallas_call(
        kernel,
        in_specs=in_specs or [ANY] * len(ins),
        out_specs=out_specs or [ANY] * len(out_shapes),
        out_shape=[jax.ShapeDtypeStruct(s, t) for s, t in out_shapes],
        scratch_shapes=scratch,
        cost_estimate=pl.CostEstimate(flops=flops, bytes_accessed=1, transcendentals=0),
        compiler_params=pltpu.CompilerParams(vmem_limit_bytes=mib * 2**20),
    )(*ins)


def run(pairs, sems, first=0):
    copies = [
        pltpu.make_async_copy(src, dst, sems.at[first + i]) for i, (src, dst) in enumerate(pairs)
    ]
    for copy in copies:
        copy.start()
    return copies


def cut_kernel(proj, part, sem):
    copy = pltpu.make_async_copy(proj.at[place(index("y"), BLOCK), :], part, sem)
    copy.start()
    copy.wait()


def cut(proj):
    return call(
        cut_kernel,
        (proj,),
        [((BLOCK, WIDTH), BF16)],
        [pltpu.SemaphoreType.DMA],
        4,
        out_specs=[VMEM],
    )[0]


def split_kernel(teacher, o1, o3, o2, sems):
    x, zh, c = (index(a) for a in ("x", "zh", "c"))
    pairs = []
    for s, out in ((1, o1), (3, o3), (2, o2)):
        for j, (zh_at, c_at) in enumerate(pieces(zh, c)):
            pairs.append(
                (
                    teacher.at[:, columns((x + s) % N, zh_at, c_at)],
                    out.at[:, pl.ds(j * WIDTH, WIDTH)],
                )
            )
    for copy in run(pairs, sems):
        copy.wait()


def split(teacher):
    return call(
        split_kernel,
        (teacher,),
        [((TOK, 4 * WIDTH), BF16)] * 3,
        [pltpu.SemaphoreType.DMA((12,))],
        8,
        BIG,
        out_specs=[VMEM] * 3,
    )


def join_kernel(own, p1, p3, lower, upper, _, out, sems):
    y = index("y")
    spots = [place((y + N - s) % N, BLOCK) for s in range(N)]
    across = pl.multiple_of((y + 2) % N * BLOCK, BLOCK)
    pairs = [
        (own, out.at[spots[0], :]),
        (p1, out.at[spots[1], :]),
        (p3, out.at[spots[3], :]),
        (lower, out.at[pl.ds(across, BLOCK // 2), :]),
        (upper, out.at[pl.ds(across + BLOCK // 2, BLOCK // 2), :]),
    ]
    for copy in run(pairs, sems):
        copy.wait()


def join(parts):
    return call(
        join_kernel,
        parts,
        [((DS, WIDTH), BF16)],
        [pltpu.SemaphoreType.DMA((5,))],
        8,
        out_specs=[VMEM],
    )[0]


def mark_kernel(*refs):
    refs[-1][...] = jnp.zeros_like(refs[-1])


def mark(values, flops):
    return call(mark_kernel, values, [((8, 128), F32)], [], 1, flops, out_specs=[VMEM])[0]


def error_kernel(half, s0, s1, s2, s3, w_own, w_other, teacher, t1, t2, t3, *rest):
    error, grad, students, weights, targets, errors, grads, sems, out_sems = rest
    x, zh, c = (index(a) for a in ("x", "zh", "c"))
    zh_at = zh if half == 0 else 1 - zh
    spots = [place((x + N - s) % N, TOK) for s in range(N)]
    first = run(
        [(ref, students.at[spot, :]) for ref, spot in zip((s0, s1, s2, s3), spots)]
        + [(w_other, weights.at[1])],
        sems,
    )
    second = run(
        [
            (ref.at[:, pl.ds(half * 2 * WIDTH, 2 * WIDTH)], targets.at[spot, :])
            for ref, spot in zip((t1, t2, t3), spots[1:])
        ]
        + [
            (
                teacher.at[:, columns(x, zh_at, c_at)],
                targets.at[spots[0], pl.ds(j * WIDTH, WIDTH)],
            )
            for j, c_at in enumerate((c, 1 - c))
        ]
        + [(w_own, weights.at[0])],
        sems,
        5,
    )
    for copy in first + second[:-1]:
        copy.wait()

    def one(j):
        def step(i, _):
            cols = pl.ds(pl.multiple_of(j * WIDTH + i * 256, 256), 256)
            predicted = dot(students[...], weights[j, :, place(i, 256)], 1, 0)
            errors[:, cols] = (predicted - targets[:, cols].astype(F32)).astype(BF16)

        lax.fori_loop(0, 2, step, None)

    one(1)
    turned = errors[:, pl.ds(WIDTH, WIDTH)].T

    def step(n, _):
        cols = place(n, BLOCK)
        grads[:, cols] = dot(turned, students[:, cols], 1, 0).astype(BF16)

    lax.fori_loop(0, N, step, None)
    out = run([(grads, grad)], out_sems)
    second[-1].wait()
    one(0)
    out += run([(errors, error)], out_sems, 1)
    for copy in out:
        copy.wait()


def error_and_other(half, students, w_own, w_other, teacher, targets):
    n_tok = N * TOK
    return call(
        functools.partial(error_kernel, half),
        (*students, w_own, w_other, teacher, *targets),
        [((n_tok, 2 * WIDTH), BF16), ((WIDTH, DS), BF16)],
        [
            pltpu.VMEM((n_tok, DS), BF16),
            pltpu.VMEM((2, DS, WIDTH), BF16),
            pltpu.VMEM((n_tok, 2 * WIDTH), BF16),
            pltpu.VMEM((n_tok, 2 * WIDTH), BF16),
            pltpu.VMEM((WIDTH, DS), BF16),
            pltpu.SemaphoreType.DMA((11,)),
            pltpu.SemaphoreType.DMA((2,)),
        ],
    18,
        BIG,
    )


def own_kernel(order, s0, s1, s2, s3, error, there, *rest):
    ins, rest = rest[: len(order) - 1], rest[len(order) - 1 :]
    outs, rest = rest[: 2 if order == (2,) else 3], rest[2 if order == (2,) else 3 :]
    students, errors, theirs, passed, grads, sems, there_sems, out_sems = rest
    x, y = index("x"), index("y")
    spots = [place((x + N - s) % N, TOK) for s in range(N)]
    begun = run([(error.at[:, pl.ds(0, WIDTH)], errors)], sems)
    begun += run([(ref, passed.at[i]) for i, ref in enumerate(ins)], sems, 13)
    loads = []
    for k, s in enumerate(order):
        cols = place((y + s) % N, BLOCK)
        loads.append(
            run(
                [
                    (ref.at[:, cols], students.at[k, spot, :])
                    for ref, spot in zip((s0, s1, s2, s3), spots)
                ],
                sems,
                1 + 4 * k,
            )
            + run([(there.at[:, cols], theirs.at[k])], there_sems, k)
        )
    for copy in begun:
        copy.wait()
    turned = errors[...].T
    out = []
    half = WIDTH // 2
    for k, s in enumerate(order):
        for copy in loads[k]:
            copy.wait()
        total = dot(turned, students[k], 1, 0) + theirs[k].astype(F32)
        if s == 1:
            grads[k, :half] = (total[:half] + passed[0].astype(F32)).astype(BF16)
            grads[k, half:] = total[half:].astype(BF16)
        elif s == 3:
            grads[k, :half] = total[:half].astype(BF16)
            grads[k, half:] = (total[half:] + passed[1].astype(F32)).astype(BF16)
        else:
            grads[k] = total.astype(BF16)
        if s == 2:
            out += run(
                [(grads.at[k, :half], outs[0]), (grads.at[k, half:], outs[1])], out_sems
            )
        else:
            out += run([(grads.at[k], outs[k])], out_sems, k)
    for copy in out:
        copy.wait()


def own_and_sum(order, students, error, there, ins=()):
    n_tok, n = N * TOK, len(order)
    halves = [((WIDTH // 2, BLOCK), BF16)] * 2
    return call(
        functools.partial(own_kernel, order),
        (*students, error, there, *ins),
        halves if order == (2,) else [((WIDTH, BLOCK), BF16)] * 3,
        [
            pltpu.VMEM((n, n_tok, BLOCK), BF16),
            pltpu.VMEM((n_tok, WIDTH), BF16),
            pltpu.VMEM((n, WIDTH, BLOCK), BF16),
            pltpu.VMEM((2, WIDTH // 2, BLOCK), BF16),
            pltpu.VMEM((n, WIDTH, BLOCK), BF16),
            pltpu.SemaphoreType.DMA((15,)),
            pltpu.SemaphoreType.DMA((3,)),
            pltpu.SemaphoreType.DMA((3,)),
        ],
        12,
    )


def student_kernel(near, far, wa, wb, wc, wd, o0, o1, o3, o2, *rest):
    errors, weights, grads, sems, out_sems = rest
    x = index("x")
    loads = run([(near, errors.at[0]), (far, errors.at[1])], sems)
    loads += run([(w, weights.at[i]) for i, w in enumerate((wa, wb, wc, wd))], sems, 2)
    for copy in loads:
        copy.wait()

    def step(n, _):
        cols = place(n, BLOCK)
        total = None
        for p in range(4):
            term = dot(errors[p // 2, :, pl.ds(p % 2 * WIDTH, WIDTH)], weights[p, cols, :], 1, 1)
            total = term if total is None else total + term
        grads[:, cols] = total.astype(BF16)

    lax.fori_loop(0, N, step, None)
    stores = run(
        [
            (grads.at[place((x + s) % N, TOK), :], out)
            for s, out in enumerate((o0, o1, o2, o3))
        ],
        out_sems,
    )
    for copy in stores:
        copy.wait()


def student_part(near, far, weights):
    n_tok = N * TOK
    return call(
        student_kernel,
        (near, far, *weights),
        [((TOK, DS), BF16)] * 4,
        [
            pltpu.VMEM((2, n_tok, 2 * WIDTH), BF16),
            pltpu.VMEM((4, DS, WIDTH), BF16),
            pltpu.VMEM((n_tok, DS), BF16),
            pltpu.SemaphoreType.DMA((6,)),
            pltpu.SemaphoreType.DMA((4,)),
        ],
        20,
        BIG,
    )


def y_kernel(a, b, c, *outs):
    zl = index("zl")
    for s, out in zip((0, 1, 3, 2), outs):
        cols = place((zl + s) % N, ROWS)
        total = a[:, cols].astype(F32) + b[:, cols].astype(F32) + c[:, cols].astype(F32)
        out[...] = total.astype(out.dtype)


def z_kernel(own, p1, p2, p3, out):
    total = own[...] + p1[...].astype(F32) + p2[...].astype(F32) + p3[...].astype(F32)
    out[...] = total.astype(BF16)


def final_kernel(own, p1, p2, p3, far, out):
    total = own[...] + p1[...].astype(F32) + p2[...].astype(F32) + p3[...].astype(F32)
    out[...] = (total + far[...].astype(F32)).T * (1.0 / math.sqrt(TOK * 256))


def student_sum_kernel(own, p1, p2, p3, out):
    total = own[...].astype(F32) + p1[...].astype(F32)
    out[...] = (total + p2[...].astype(F32) + p3[...].astype(F32)).astype(BF16)


def in_vmem(kernel, ins, outs, flops=1):
    return call(kernel, ins, outs, [], 8, flops, in_specs=[VMEM] * len(ins), out_specs=[VMEM] * len(outs))


def over(axis, blocks, *done):
    got = {s: shift(after(b, *done), axis, s) for s, b in zip((1, 3, 2), blocks)}
    return [got[s] for s in (1, 2, 3)]


def body(teacher, student, proj):
    students = [student] + over("x", [student] * 3)
    part = shift(cut(proj), "zh", 1)
    proj_b = shift(proj, "c", 1)
    sends = split(after(teacher, *students[1:], proj_b))
    targets = over("x", sends)

    p1, p3 = (shift(after(part, *sends), "y", s) for s in (1, 3))
    lower, upper = shift(p1[: BLOCK // 2], "y", 1), shift(p3[BLOCK // 2 :], "y", 3)
    proj_c = join([part, p1, p3, lower, upper, mark(targets, SMALL)])
    proj_d = shift(proj_c, "c", 1)

    near, there = error_and_other(0, students, after(proj, proj_c), proj_b, teacher, targets)
    near_there = shift(there, "c", 1)
    far, there = error_and_other(1, students, after(proj_c, near), proj_d, teacher, targets)
    far_there = shift(there, "c", 1)

    blocks = own_and_sum((2,), students, near, after(near_there, far))
    near_in = [shift(blocks[0], "y", 1), shift(blocks[1], "y", 3)]
    blocks = own_and_sum((2,), students, far, after(far_there, *blocks))
    far_in = [shift(blocks[0], "y", 1), shift(blocks[1], "y", 3)]
    near_sum = own_and_sum((1, 3, 0), students, near, after(near_there, *blocks), near_in)
    near_y = [near_sum[2], shift(near_sum[0], "y", 1), shift(near_sum[1], "y", 3)]
    weights = (proj, proj_b, proj_c, after(proj_d, *far_in, near_sum[2]))
    partial = student_part(near, far, weights)
    back2 = shift(partial[3], "x", 2)
    far_sum = own_and_sum((1, 3, 0), students, far, after(far_there, partial[0]), far_in)
    ready = [after(b, *near_y[1:]) for b in far_sum[:2]]
    far_y = [far_sum[2], shift(ready[0], "y", 1), shift(ready[1], "y", 3)]

    def over_y(terms):
        return in_vmem(
            y_kernel, terms, [((WIDTH, ROWS), F32)] + [((WIDTH, ROWS), BF16)] * 3, BIG
        )

    near_z = over_y([after(near_y[0], *far_sum), *near_y[1:]])
    near_terms = [near_z[0]] + over("zl", near_z[1:])
    far_z = over_y([after(far_y[0], back2, *near_terms), *far_y[1:]])
    far_terms = [far_z[0]] + over("zl", far_z[1:])
    back1 = shift(after(partial[1], *far_z), "x", 1)
    back3 = shift(after(partial[2], *far_z), "x", 3)
    far_part = in_vmem(
        z_kernel, [after(far_terms[0], back1, back3), *far_terms[1:]], [((WIDTH, ROWS), BF16)]
    )[0]
    far_part = shift(far_part, "zh", 1)
    grad_student = in_vmem(
        student_sum_kernel, [partial[0], back1, back2, back3], [((TOK, DS), BF16)]
    )[0]
    grad_proj = in_vmem(final_kernel, [*near_terms, far_part], [((ROWS, WIDTH), F32)])[0]
    return grad_proj, grad_student


def solution(mesh):
    fine = Mesh(mesh.devices.reshape(4, 4, 4, 2, 2), ALL)
    tokens = P(ALL, None)
    return jax.shard_map(
        body,
        mesh=fine,
        in_specs=(tokens, tokens, P(None, ("x", "zh", "c"))),
        out_specs=(P(("y", "zl"), ("x", "zh", "c")), tokens),
        check_vma=False,
    )
```

```python
import functools
import math

import jax
import jax.numpy as jnp
from jax import lax
from jax.experimental import pallas as pl
from jax.experimental.pallas import tpu as pltpu
from jax.sharding import Mesh
from jax.sharding import PartitionSpec as P

F32 = jnp.float32
BF16 = jnp.bfloat16
ALL = ("y", "zl", "x", "zh", "c")
ANY = pl.BlockSpec(memory_space=pl.ANY)
VMEM = pl.BlockSpec(memory_space=pltpu.VMEM)
N = 4
TOK, DS, WIDTH = 128, 2048, 512
BLOCK = DS // N
ROWS = BLOCK // N
BIG = 10**11
SMALL = 3 * 10**8
REST = 16


def shift(array, axis, by):
    n = lax.axis_size(axis)
    return lax.ppermute(array, axis, [(i, (i + by) % n) for i in range(n)])


def after(value, *done):
    return lax.optimization_barrier((*done, value))[-1]


def index(axis):
    return lax.axis_index(axis)


def columns(x_at, zh_at, c_at):
    return pl.ds(pl.multiple_of(((x_at * 2 + zh_at) * 2 + c_at) * WIDTH, WIDTH), WIDTH)


def place(at, size):
    return pl.ds(pl.multiple_of(at * size, size), size)


def pieces(zh, c):
    return ((zh, c), (zh, 1 - c), (1 - zh, c), (1 - zh, 1 - c))


def dot(a, b, da, db):
    return lax.dot_general(a, b, (((da,), (db,)), ((), ())), preferred_element_type=F32)


def call(kernel, ins, out_shapes, scratch, mib, flops=1, out_specs=None, in_specs=None):
    return pl.pallas_call(
        kernel,
        in_specs=in_specs or [ANY] * len(ins),
        out_specs=out_specs or [ANY] * len(out_shapes),
        out_shape=[jax.ShapeDtypeStruct(s, t) for s, t in out_shapes],
        scratch_shapes=scratch,
        cost_estimate=pl.CostEstimate(flops=flops, bytes_accessed=1, transcendentals=0),
        compiler_params=pltpu.CompilerParams(vmem_limit_bytes=mib * 2**20),
    )(*ins)


def run(pairs, sems, first=0):
    copies = [
        pltpu.make_async_copy(src, dst, sems.at[first + i]) for i, (src, dst) in enumerate(pairs)
    ]
    for copy in copies:
        copy.start()
    return copies


def cut_kernel(proj, part, sem):
    copy = pltpu.make_async_copy(proj.at[place(index("y"), BLOCK), :], part, sem)
    copy.start()
    copy.wait()


def cut(proj):
    return call(
        cut_kernel,
        (proj,),
        [((BLOCK, WIDTH), BF16)],
        [pltpu.SemaphoreType.DMA],
        4,
        out_specs=[VMEM],
    )[0]


def split_kernel(teacher, student, o1, o3, o2, sems):
    x, zh, c = (index(a) for a in ("x", "zh", "c"))
    pairs = []
    for s, out in ((1, o1), (3, o3), (2, o2)):
        pairs.append((student, out.at[pl.ds(TOK, TOK), :]))
        for j, (zh_at, c_at) in enumerate(pieces(zh, c)):
            pairs.append(
                (
                    teacher.at[:, columns((x + s) % N, zh_at, c_at)],
                    out.at[pl.ds(0, TOK), pl.ds(j * WIDTH, WIDTH)],
                )
            )
    for copy in run(pairs, sems):
        copy.wait()


def split(teacher, student):
    return call(
        split_kernel,
        (teacher, student),
        [((2 * TOK, 4 * WIDTH), BF16)] * 3,
        [pltpu.SemaphoreType.DMA((15,))],
        8,
        out_specs=[VMEM] * 3,
    )


def relay_kernel(part, p1, p3, lower, upper, sems):
    half = BLOCK // 2
    pairs = [
        (p1.at[:half, :], lower.at[:half, :]),
        (part.at[BLOCK - REST :, :], lower.at[half:, :]),
        (p3.at[half - REST :, :], upper.at[:half, :]),
        (part.at[:REST, :], upper.at[half:, :]),
    ]
    for copy in run(pairs, sems):
        copy.wait()


def relay(*ins):
    return call(
        relay_kernel,
        ins,
        [((BLOCK // 2 + REST, WIDTH), BF16)] * 2,
        [pltpu.SemaphoreType.DMA((4,))],
        4,
        out_specs=[VMEM] * 2,
    )


def join_kernel(own, p1, p3, lower, upper, _, out, sems):
    y = index("y")
    half = BLOCK // 2

    def rows(s, first, size):
        return out.at[pl.ds(pl.multiple_of((y + N - s) % N * BLOCK + first, REST), size), :]

    pairs = [
        (own, rows(0, 0, BLOCK)),
        (p1, rows(1, 0, BLOCK - REST)),
        (p3, rows(3, REST, BLOCK - REST)),
        (lower.at[:half, :], rows(2, 0, half)),
        (lower.at[half:, :], rows(1, BLOCK - REST, REST)),
        (upper.at[:half, :], rows(2, half, half)),
        (upper.at[half:, :], rows(3, 0, REST)),
    ]
    for copy in run(pairs, sems):
        copy.wait()


def join(parts):
    return call(
        join_kernel,
        parts,
        [((DS, WIDTH), BF16)],
        [pltpu.SemaphoreType.DMA((7,))],
        8,
        out_specs=[VMEM],
    )[0]


def mark_kernel(*refs):
    refs[-1][...] = jnp.zeros_like(refs[-1])


def mark(values, flops):
    return call(mark_kernel, values, [((8, 128), F32)], [], 1, flops, out_specs=[VMEM])[0]


def error_kernel(half, student, b1, b2, b3, w_own, w_other, teacher, errors, grads, *rest):
    students, targets, sems = rest
    x, zh, c = (index(a) for a in ("x", "zh", "c"))
    zh_at = zh if half == 0 else 1 - zh
    blocks = (b1, b2, b3)
    rows = [pl.ds(s * TOK, TOK) for s in range(N)]
    loads = run(
        [(student, students.at[rows[0], :])]
        + [(block.at[rows[1], :], students.at[row, :]) for block, row in zip(blocks, rows[1:])]
        + [
            (teacher.at[:, columns(x, zh_at, c_at)], targets.at[:, pl.ds(j * WIDTH, WIDTH)])
            for j, c_at in enumerate((c, 1 - c))
        ],
        sems,
    )
    for copy in loads:
        copy.wait()

    def one(j, weights):
        def step(i, _):
            here = j * WIDTH + i * 256
            cols = pl.ds(pl.multiple_of(here, 256), 256)
            away = pl.ds(pl.multiple_of(half * 2 * WIDTH + here, 256), 256)
            predicted = dot(students[...], weights[:, place(i, 256)], 1, 0)
            for s in range(N):
                target = targets[:, cols] if s == 0 else blocks[s - 1][rows[0], away]
                part = predicted[s * TOK : (s + 1) * TOK] - target.astype(F32)
                errors[rows[s], cols] = part.astype(BF16)

        lax.fori_loop(0, 2, step, None)

    one(1, w_other)
    turned = errors[:, pl.ds(WIDTH, WIDTH)].T

    def step(n, _):
        cols = place(n, BLOCK)
        grads[:, cols] = dot(turned, students[:, cols], 1, 0).astype(BF16)

    lax.fori_loop(0, N, step, None)
    one(0, w_own)


def error_and_other(half, student, blocks, w_own, w_other, teacher):
    n_tok = N * TOK
    return call(
        functools.partial(error_kernel, half),
        (student, *blocks, w_own, w_other, teacher),
        [((n_tok, 2 * WIDTH), BF16), ((WIDTH, DS), BF16)],
        [
            pltpu.VMEM((n_tok, DS), BF16),
            pltpu.VMEM((TOK, 2 * WIDTH), BF16),
            pltpu.SemaphoreType.DMA((6,)),
        ],
        12,
        BIG,
        in_specs=[ANY] + [VMEM] * 5 + [ANY],
        out_specs=[VMEM] * 2,
    )


def own_kernel(order, student, b1, b2, b3, error, there, *rest):
    ins, rest = rest[: len(order) - 1], rest[len(order) - 1 :]
    *outs, students, sems = rest
    y = index("y")
    held = (student, *(block.at[pl.ds(TOK, TOK), :] for block in (b1, b2, b3)))
    spots = [place((y + s) % N, BLOCK) for s in order]
    loads = [
        run(
            [
                (ref.at[:, spot], students.at[k, pl.ds(s * TOK, TOK), :])
                for s, ref in enumerate(held)
            ],
            sems,
            4 * k,
        )
        for k, spot in enumerate(spots)
    ]
    turned = error[:, pl.ds(0, WIDTH)].T
    half = WIDTH // 2
    for k, s in enumerate(order):
        for copy in loads[k]:
            copy.wait()
        total = dot(turned, students[k], 1, 0) + there[:, spots[k]].astype(F32)
        low, high = total[:half], total[half:]
        if s == 1:
            low = low + ins[0][...].astype(F32)
        elif s == 3:
            high = high + ins[1][...].astype(F32)
        if s == 2:
            outs[0][...] = low.astype(BF16)
            outs[1][...] = high.astype(BF16)
        else:
            outs[k][:half] = low.astype(BF16)
            outs[k][half:] = high.astype(BF16)


def own_and_sum(order, students, error, there, ins=(), flops=1):
    n_tok, n = N * TOK, len(order)
    halves = [((WIDTH // 2, BLOCK), BF16)] * 2
    outs = halves if order == (2,) else [((WIDTH, BLOCK), BF16)] * 3
    return call(
        functools.partial(own_kernel, order),
        (*students, error, there, *ins),
        outs,
        [pltpu.VMEM((n, n_tok, BLOCK), BF16), pltpu.SemaphoreType.DMA((4 * n,))],
        10,
        flops,
        in_specs=[ANY] * 4 + [VMEM] * (2 + len(ins)),
        out_specs=[VMEM] * len(outs),
    )


def student_kernel(near, far, wa, wb, wc, wd, o0, o1, o3, low, high):
    errors, weights = (near, far), (wa, wb, wc, wd)

    def step(n, _):
        cols = place(n, BLOCK)
        total = None
        for p in range(4):
            term = dot(errors[p // 2][:, pl.ds(p % 2 * WIDTH, WIDTH)], weights[p][cols, :], 1, 1)
            total = term if total is None else total + term
        for s, out in ((0, o0), (1, o3), (3, o1)):
            out[:, cols] = total[s * TOK : (s + 1) * TOK].astype(BF16)
        low[:, cols] = total[2 * TOK : 2 * TOK + TOK // 2].astype(BF16)
        high[:, cols] = total[2 * TOK + TOK // 2 : 3 * TOK].astype(BF16)

    lax.fori_loop(0, N, step, None)


def student_part(near, far, weights):
    return call(
        student_kernel,
        (near, far, *weights),
        [((TOK, DS), BF16)] * 3 + [((TOK // 2, DS), BF16)] * 2,
        [],
        12,
        BIG,
        in_specs=[VMEM] * 6,
        out_specs=[VMEM] * 5,
    )


def pass_kernel(b1, b3, low, high, o1, o3):
    half = TOK // 2
    o1[:half] = (b1[:half].astype(F32) + low[...].astype(F32)).astype(BF16)
    o1[half:] = b1[half:]
    o3[:half] = b3[:half]
    o3[half:] = (b3[half:].astype(F32) + high[...].astype(F32)).astype(BF16)


def y_kernel(a, b, c, *outs):
    zl = index("zl")
    for s, out in zip((0, 1, 3, 2), outs):
        cols = place((zl + s) % N, ROWS)
        total = a[:, cols].astype(F32) + b[:, cols].astype(F32) + c[:, cols].astype(F32)
        out[...] = total.astype(out.dtype)


def z_kernel(own, p1, p2, p3, out):
    total = own[...] + p1[...].astype(F32) + p2[...].astype(F32) + p3[...].astype(F32)
    out[...] = total.astype(BF16)


def final_kernel(own, p1, p2, p3, far, out):
    total = own[...] + p1[...].astype(F32) + p2[...].astype(F32) + p3[...].astype(F32)
    out[...] = (total + far[...].astype(F32)).T * (1.0 / math.sqrt(TOK * 256))


def student_sum_kernel(own, p1, p3, out):
    total = own[...].astype(F32) + p1[...].astype(F32)
    out[...] = (total + p3[...].astype(F32)).astype(BF16)


def in_vmem(kernel, ins, outs, flops=1):
    return call(kernel, ins, outs, [], 8, flops, in_specs=[VMEM] * len(ins), out_specs=[VMEM] * len(outs))


def over(axis, blocks, *done):
    got = {s: shift(after(b, *done), axis, s) for s, b in zip((1, 3, 2), blocks)}
    return [got[s] for s in (1, 2, 3)]


def body(teacher, student, proj):
    blocks = over("x", split(teacher, student))
    students = (student, *blocks)
    proj_b = shift(proj, "c", 1)
    part = after(shift(cut(proj), "zh", 1), proj_b)

    p1 = shift(part[: BLOCK - REST], "y", 1)
    p3 = shift(part[REST:], "y", 3)
    lower, upper = relay(part, p1, p3)
    lower, upper = shift(lower, "y", 1), shift(upper, "y", 3)
    proj_c = join([part, p1, p3, lower, upper, mark(blocks, SMALL)])
    proj_d = shift(proj_c, "c", 1)

    near, there = error_and_other(0, student, blocks, after(proj, proj_c), proj_b, teacher)
    near_there = shift(there, "c", 1)
    far, there = error_and_other(1, student, blocks, after(proj_c, near), proj_d, teacher)
    far_there = shift(there, "c", 1)

    sent = own_and_sum((2,), students, near, after(near_there, far))
    near_in = [shift(sent[0], "y", 1), shift(sent[1], "y", 3)]
    sent = own_and_sum((2,), students, far, after(far_there, *sent))
    far_in = [shift(sent[0], "y", 1), shift(sent[1], "y", 3)]
    weights = (proj, proj_b, proj_c, after(proj_d, *sent))
    partial = student_part(near, far, weights)
    far_sum = own_and_sum(
        (1, 3, 0), students, far, after(far_there, partial[0], *near_in), far_in
    )
    passed = shift(partial[3], "x", 1), shift(partial[4], "x", 3)
    back = in_vmem(pass_kernel, [*partial[1:3], *passed], [((TOK, DS), BF16)] * 2, BIG)
    back = shift(after(back[0], far_sum[2]), "x", 1), shift(after(back[1], far_sum[2]), "x", 3)
    far_y = [far_sum[2], shift(far_sum[0], "y", 1), shift(far_sum[1], "y", 3)]
    near_sum = own_and_sum(
        (1, 3, 0), students, near, after(near_there, *far_sum), near_in
    )
    sent = [after(b, *far_y[1:]) for b in near_sum[:2]]
    near_y = [near_sum[2], shift(sent[0], "y", 1), shift(sent[1], "y", 3)]

    def over_y(terms, flops):
        outs = [((WIDTH, ROWS), F32)] + [((WIDTH, ROWS), BF16)] * 3
        return in_vmem(y_kernel, terms, outs, flops)

    far_z = over_y(far_y, 1)
    far_terms = [far_z[0]] + over("zl", far_z[1:])
    far_terms = [after(far_terms[0], *back), *far_terms[1:]]
    far_part = in_vmem(z_kernel, far_terms, [((WIDTH, ROWS), BF16)])[0]
    near_z = over_y(near_y, BIG)
    far_part = shift(after(far_part, *near_z), "zh", 1)
    near_terms = [near_z[0]] + over("zl", near_z[1:])
    grad_student = in_vmem(
        student_sum_kernel, [partial[0], *back], [((TOK, DS), BF16)]
    )[0]
    grad_proj = in_vmem(final_kernel, [*near_terms, far_part], [((ROWS, WIDTH), F32)])[0]
    return grad_proj, grad_student


def solution(mesh):
    fine = Mesh(mesh.devices.reshape(4, 4, 4, 2, 2), ALL)
    tokens = P(ALL, None)
    return jax.shard_map(
        body,
        mesh=fine,
        in_specs=(tokens, tokens, P(None, ("x", "zh", "c"))),
        out_specs=(P(("y", "zl"), ("x", "zh", "c")), tokens),
        check_vma=False,
    )
```

```python
import functools
import math

import jax
import jax.numpy as jnp
from jax import lax
from jax.experimental import pallas as pl
from jax.experimental.pallas import tpu as pltpu
from jax.sharding import Mesh
from jax.sharding import PartitionSpec as P

F32 = jnp.float32
BF16 = jnp.bfloat16
ALL = ("y", "zl", "x", "zh", "c")
ANY = pl.BlockSpec(memory_space=pl.ANY)
VMEM = pl.BlockSpec(memory_space=pltpu.VMEM)
N = 4
TOK, DS, WIDTH = 128, 2048, 512
BLOCK = DS // N
ROWS = BLOCK // N
BIG = 10**11
SMALL = 3 * 10**8
MEDIUM = 5 * 10**9


def shift(array, axis, by):
    n = lax.axis_size(axis)
    return lax.ppermute(array, axis, [(i, (i + by) % n) for i in range(n)])


def swap(array, bit):
    return lax.ppermute(array, "zl", [(i, i ^ bit) for i in range(N)])


def after(value, *done):
    return lax.optimization_barrier((*done, value))[-1]


def index(axis):
    return lax.axis_index(axis)


def columns(x_at, zh_at, c_at):
    return pl.ds(pl.multiple_of(((x_at * 2 + zh_at) * 2 + c_at) * WIDTH, WIDTH), WIDTH)


def place(at, size):
    return pl.ds(pl.multiple_of(at * size, size), size)


def pieces(zh, c):
    return ((zh, c), (zh, 1 - c), (1 - zh, c), (1 - zh, 1 - c))


def dot(a, b, da, db):
    return lax.dot_general(a, b, (((da,), (db,)), ((), ())), preferred_element_type=F32)


def call(kernel, ins, out_shapes, scratch, mib, flops=1, out_specs=None, in_specs=None):
    return pl.pallas_call(
        kernel,
        in_specs=in_specs or [ANY] * len(ins),
        out_specs=out_specs or [ANY] * len(out_shapes),
        out_shape=[jax.ShapeDtypeStruct(s, t) for s, t in out_shapes],
        scratch_shapes=scratch,
        cost_estimate=pl.CostEstimate(flops=flops, bytes_accessed=1, transcendentals=0),
        compiler_params=pltpu.CompilerParams(vmem_limit_bytes=mib * 2**20),
    )(*ins)


def run(pairs, sems, first=0):
    copies = [
        pltpu.make_async_copy(src, dst, sems.at[first + i]) for i, (src, dst) in enumerate(pairs)
    ]
    for copy in copies:
        copy.start()
    return copies


def cut_kernel(proj, part, sem):
    copy = pltpu.make_async_copy(proj.at[place(index("y"), BLOCK), :], part, sem)
    copy.start()
    copy.wait()


def cut(proj):
    return call(
        cut_kernel,
        (proj,),
        [((BLOCK, WIDTH), BF16)],
        [pltpu.SemaphoreType.DMA],
        4,
        out_specs=[VMEM],
    )[0]


def split_kernel(teacher, student, o1, o3, o2, sems):
    x, zh, c = (index(a) for a in ("x", "zh", "c"))
    pairs = []
    for s, out in ((1, o1), (3, o3), (2, o2)):
        pairs.append((student, out.at[pl.ds(TOK, TOK), :]))
        for j, (zh_at, c_at) in enumerate(pieces(zh, c)):
            pairs.append(
                (
                    teacher.at[:, columns((x + s) % N, zh_at, c_at)],
                    out.at[pl.ds(0, TOK), pl.ds(j * WIDTH, WIDTH)],
                )
            )
    for copy in run(pairs, sems):
        copy.wait()


def split(teacher, student):
    return call(
        split_kernel,
        (teacher, student),
        [((2 * TOK, 4 * WIDTH), BF16)] * 3,
        [pltpu.SemaphoreType.DMA((15,))],
        8,
        out_specs=[VMEM] * 3,
    )


def relay_kernel(p1, p3, lower, upper, sems):
    half = BLOCK // 2
    for copy in run([(p1.at[:half, :], lower), (p3.at[half:, :], upper)], sems):
        copy.wait()


def relay(*ins):
    return call(
        relay_kernel,
        ins,
        [((BLOCK // 2, WIDTH), BF16)] * 2,
        [pltpu.SemaphoreType.DMA((2,))],
        4,
        out_specs=[VMEM] * 2,
    )


def join_kernel(own, p1, p3, lower, upper, _, out, sems):
    y = index("y")
    half = BLOCK // 2

    def rows(s, first, size):
        return out.at[pl.ds(pl.multiple_of((y + N - s) % N * BLOCK + first, half), size), :]

    pairs = [
        (own, rows(0, 0, BLOCK)),
        (p1, rows(1, 0, BLOCK)),
        (p3, rows(3, 0, BLOCK)),
        (lower, rows(2, 0, half)),
        (upper, rows(2, half, half)),
    ]
    for copy in run(pairs, sems):
        copy.wait()


def join(parts):
    return call(
        join_kernel,
        parts,
        [((DS, WIDTH), BF16)],
        [pltpu.SemaphoreType.DMA((5,))],
        8,
        out_specs=[VMEM],
    )[0]


def mark_kernel(*refs):
    refs[-1][...] = jnp.zeros_like(refs[-1])


def mark(values, flops):
    return call(mark_kernel, values, [((8, 128), F32)], [], 1, flops, out_specs=[VMEM])[0]


def error_kernel(half, student, b1, b2, b3, w_own, w_other, teacher, errors, grads, *rest):
    students, targets, sems = rest
    x, zh, c = (index(a) for a in ("x", "zh", "c"))
    zh_at = zh if half == 0 else 1 - zh
    blocks = (b1, b2, b3)
    rows = [pl.ds(s * TOK, TOK) for s in range(N)]
    loads = run(
        [(student, students.at[rows[0], :])]
        + [(block.at[rows[1], :], students.at[row, :]) for block, row in zip(blocks, rows[1:])]
        + [
            (teacher.at[:, columns(x, zh_at, c_at)], targets.at[:, pl.ds(j * WIDTH, WIDTH)])
            for j, c_at in enumerate((c, 1 - c))
        ],
        sems,
    )
    for copy in loads:
        copy.wait()

    def one(j, weights):
        def step(i, _):
            here = j * WIDTH + i * 256
            cols = pl.ds(pl.multiple_of(here, 256), 256)
            away = pl.ds(pl.multiple_of(half * 2 * WIDTH + here, 256), 256)
            predicted = dot(students[...], weights[:, place(i, 256)], 1, 0)
            for s in range(N):
                target = targets[:, cols] if s == 0 else blocks[s - 1][rows[0], away]
                part = predicted[s * TOK : (s + 1) * TOK] - target.astype(F32)
                errors[rows[s], cols] = part.astype(BF16)

        lax.fori_loop(0, 2, step, None)

    one(1, w_other)
    turned = errors[:, pl.ds(WIDTH, WIDTH)].T

    def step(n, _):
        cols = place(n, BLOCK)
        grads[:, cols] = dot(turned, students[:, cols], 1, 0).astype(BF16)

    lax.fori_loop(0, N, step, None)
    one(0, w_own)


def error_and_other(half, student, blocks, w_own, w_other, teacher):
    n_tok = N * TOK
    return call(
        functools.partial(error_kernel, half),
        (student, *blocks, w_own, w_other, teacher),
        [((n_tok, 2 * WIDTH), BF16), ((WIDTH, DS), BF16)],
        [
            pltpu.VMEM((n_tok, DS), BF16),
            pltpu.VMEM((TOK, 2 * WIDTH), BF16),
            pltpu.SemaphoreType.DMA((6,)),
        ],
        12,
        BIG,
        in_specs=[ANY] + [VMEM] * 5 + [ANY],
        out_specs=[VMEM] * 2,
    )


def own_kernel(order, n_in, student, b1, b2, b3, error, there, *rest):
    ins, rest = rest[:n_in], rest[n_in:]
    *outs, students, sems = rest
    y = index("y")
    held = (student, *(block.at[pl.ds(TOK, TOK), :] for block in (b1, b2, b3)))
    spots = [place((y + s) % N, BLOCK) for s in order]
    loads = [
        run(
            [
                (ref.at[:, spot], students.at[k, pl.ds(s * TOK, TOK), :])
                for s, ref in enumerate(held)
            ],
            sems,
            4 * k,
        )
        for k, spot in enumerate(spots)
    ]
    turned = error[:, pl.ds(0, WIDTH)].T
    half = WIDTH // 2
    for k, s in enumerate(order):
        for copy in loads[k]:
            copy.wait()
        total = dot(turned, students[k], 1, 0) + there[:, spots[k]].astype(F32)
        low, high = total[:half], total[half:]
        if ins and s == 1:
            low = low + ins[0][...].astype(F32)
        elif ins and s == 3:
            high = high + ins[1][...].astype(F32)
        if s == 2:
            outs[0][...] = low.astype(BF16)
            outs[1][...] = high.astype(BF16)
        else:
            outs[k][:half] = low.astype(BF16)
            outs[k][half:] = high.astype(BF16)


def own_and_sum(order, students, error, there, ins=(), flops=1):
    n_tok, n = N * TOK, len(order)
    halves = [((WIDTH // 2, BLOCK), BF16)] * 2
    outs = halves if order == (2,) else [((WIDTH, BLOCK), BF16)] * 3
    return call(
        functools.partial(own_kernel, order, len(ins)),
        (*students, error, there, *ins),
        outs,
        [pltpu.VMEM((n, n_tok, BLOCK), BF16), pltpu.SemaphoreType.DMA((4 * n,))],
        10,
        flops,
        in_specs=[ANY] * 4 + [VMEM] * (2 + len(ins)),
        out_specs=[VMEM] * len(outs),
    )


def student_kernel(near, far, wa, wb, wc, wd, o0, o1, o3, low, high):
    errors, weights = (near, far), (wa, wb, wc, wd)

    def step(n, _):
        cols = place(n, BLOCK)
        total = None
        for p in range(4):
            term = dot(errors[p // 2][:, pl.ds(p % 2 * WIDTH, WIDTH)], weights[p][cols, :], 1, 1)
            total = term if total is None else total + term
        for s, out in ((0, o0), (1, o3), (3, o1)):
            out[:, cols] = total[s * TOK : (s + 1) * TOK].astype(BF16)
        low[:, cols] = total[2 * TOK : 2 * TOK + TOK // 2].astype(BF16)
        high[:, cols] = total[2 * TOK + TOK // 2 : 3 * TOK].astype(BF16)

    lax.fori_loop(0, N, step, None)


def student_part(near, far, weights):
    return call(
        student_kernel,
        (near, far, *weights),
        [((TOK, DS), BF16)] * 3 + [((TOK // 2, DS), BF16)] * 2,
        [],
        12,
        BIG,
        in_specs=[VMEM] * 6,
        out_specs=[VMEM] * 5,
    )


def pass_kernel(b1, b3, low, high, o1, o3):
    half = b1.shape[0] // 2
    o1[:half] = (b1[:half].astype(F32) + low[...].astype(F32)).astype(BF16)
    o1[half:] = b1[half:]
    o3[:half] = b3[:half]
    o3[half:] = (b3[half:].astype(F32) + high[...].astype(F32)).astype(BF16)


def y_kernel(a, b, c, own, other, out):
    zl = index("zl")

    def block(at):
        cols = place(at, ROWS)
        return a[:, cols].astype(F32) + b[:, cols].astype(F32) + c[:, cols].astype(F32)

    own[...] = block(zl)
    other[...] = block(zl ^ 2)
    out[:, :ROWS] = block(zl ^ 1).astype(BF16)
    out[:, ROWS:] = block(zl ^ 3).astype(BF16)


def pair_kernel(own, other, got, total, out):
    total[...] = own[...] + got[:, :ROWS].astype(F32)
    out[...] = (other[...] + got[:, ROWS:].astype(F32)).astype(BF16)


def z_kernel(own, got, out):
    out[...] = (own[...] + got[...].astype(F32)).astype(BF16)


def final_kernel(own, got, far, out):
    total = own[...] + got[...].astype(F32) + far[...].astype(F32)
    out[...] = total.T * (1.0 / math.sqrt(TOK * 256))


def student_sum_kernel(own, p1, p3, out):
    total = own[...].astype(F32) + p1[...].astype(F32)
    out[...] = (total + p3[...].astype(F32)).astype(BF16)


def in_vmem(kernel, ins, outs, flops=1):
    return call(kernel, ins, outs, [], 8, flops, in_specs=[VMEM] * len(ins), out_specs=[VMEM] * len(outs))


def over(axis, blocks, *done):
    got = {s: shift(after(b, *done), axis, s) for s, b in zip((1, 3, 2), blocks)}
    return [got[s] for s in (1, 2, 3)]


def body(teacher, student, proj):
    blocks = over("x", split(teacher, student))
    students = (student, *blocks)
    proj_b = shift(proj, "c", 1)
    part = after(shift(cut(proj), "zh", 1), proj_b)

    p1, p3 = shift(part, "y", 1), shift(part, "y", 3)
    lower, upper = relay(p1, p3)
    lower, upper = shift(lower, "y", 1), shift(upper, "y", 3)
    proj_c = join([part, p1, p3, lower, upper, mark(blocks, SMALL)])
    proj_d = shift(proj_c, "c", 1)

    near, there = error_and_other(0, student, blocks, after(proj, proj_c), proj_b, teacher)
    near_there = shift(there, "c", 1)
    far, there = error_and_other(1, student, blocks, after(proj_c, near), proj_d, teacher)
    far_there = shift(there, "c", 1)

    sent = own_and_sum((2,), students, near, after(near_there, far))
    near_in = [shift(sent[0], "y", 1), shift(sent[1], "y", 3)]
    sent = own_and_sum((2,), students, far, after(far_there, *sent))
    far_in = [shift(sent[0], "y", 1), shift(sent[1], "y", 3)]
    far_sum = own_and_sum((1, 3, 0), students, far, after(far_there, *sent))
    weights = (proj, proj_b, proj_c, after(proj_d, *far_sum))
    partial = student_part(near, far, weights)
    terms = [*far_sum[:2], after(far_in[0], partial[0], *near_in), far_in[1]]
    ready = in_vmem(pass_kernel, terms, [((WIDTH, BLOCK), BF16)] * 2)
    passed = shift(partial[3], "x", 1), shift(partial[4], "x", 3)
    back = in_vmem(pass_kernel, [*partial[1:3], *passed], [((TOK, DS), BF16)] * 2, BIG)
    back = shift(after(back[0], ready[0]), "x", 1), shift(after(back[1], ready[0]), "x", 3)
    far_y = [far_sum[2], shift(ready[0], "y", 1), shift(ready[1], "y", 3)]
    near_sum = own_and_sum(
        (1, 3, 0), students, near, after(near_there, *ready), near_in
    )
    sent = [after(b, *far_y[1:]) for b in near_sum[:2]]
    near_y = [near_sum[2], shift(sent[0], "y", 1), shift(sent[1], "y", 3)]

    def over_y_and_pair(terms, flops):
        outs = [((WIDTH, ROWS), F32)] * 2 + [((WIDTH, 2 * ROWS), BF16)]
        own, other, out = in_vmem(y_kernel, terms, outs, flops)
        outs = [((WIDTH, ROWS), F32), ((WIDTH, ROWS), BF16)]
        own, out = in_vmem(pair_kernel, [own, other, swap(out, 1)], outs)
        return [own, swap(out, 2)]

    far_terms = over_y_and_pair(far_y, 1)
    far_terms = [after(far_terms[0], *back), far_terms[1]]
    far_part = in_vmem(z_kernel, far_terms, [((WIDTH, ROWS), BF16)], MEDIUM)[0]
    near_terms = over_y_and_pair(near_y, BIG)
    far_part = shift(far_part, "zh", 1)
    grad_student = in_vmem(
        student_sum_kernel, [partial[0], *back], [((TOK, DS), BF16)]
    )[0]
    grad_proj = in_vmem(final_kernel, [*near_terms, far_part], [((ROWS, WIDTH), F32)])[0]
    return grad_proj, grad_student


def solution(mesh):
    fine = Mesh(mesh.devices.reshape(4, 4, 4, 2, 2), ALL)
    tokens = P(ALL, None)
    return jax.shard_map(
        body,
        mesh=fine,
        in_specs=(tokens, tokens, P(None, ("x", "zh", "c"))),
        out_specs=(P(("y", "zl"), ("x", "zh", "c")), tokens),
        check_vma=False,
    )
```

```python
import functools
import math

import jax
import jax.numpy as jnp
from jax import lax
from jax.experimental import pallas as pl
from jax.experimental.pallas import tpu as pltpu
from jax.sharding import Mesh
from jax.sharding import PartitionSpec as P

F32 = jnp.float32
BF16 = jnp.bfloat16
ALL = ("y", "zl", "x", "zh", "c")
ANY = pl.BlockSpec(memory_space=pl.ANY)
VMEM = pl.BlockSpec(memory_space=pltpu.VMEM)
N = 4
TOK, DS, WIDTH = 128, 2048, 512
BLOCK = DS // N
ROWS = BLOCK // N
BIG = 10**11
SMALL = 3 * 10**8
MEDIUM = 5 * 10**9


def shift(array, axis, by):
    n = lax.axis_size(axis)
    return lax.ppermute(array, axis, [(i, (i + by) % n) for i in range(n)])


def swap(array, bit):
    return lax.ppermute(array, "zl", [(i, i ^ bit) for i in range(N)])


def after(value, *done):
    return lax.optimization_barrier((*done, value))[-1]


def index(axis):
    return lax.axis_index(axis)


def columns(x_at, zh_at, c_at):
    return pl.ds(pl.multiple_of(((x_at * 2 + zh_at) * 2 + c_at) * WIDTH, WIDTH), WIDTH)


def place(at, size):
    return pl.ds(pl.multiple_of(at * size, size), size)


def pieces(zh, c):
    return ((zh, c), (zh, 1 - c), (1 - zh, c), (1 - zh, 1 - c))


def dot(a, b, da, db):
    return lax.dot_general(a, b, (((da,), (db,)), ((), ())), preferred_element_type=F32)


def call(kernel, ins, out_shapes, scratch, mib, flops=1, out_specs=None, in_specs=None):
    return pl.pallas_call(
        kernel,
        in_specs=in_specs or [ANY] * len(ins),
        out_specs=out_specs or [ANY] * len(out_shapes),
        out_shape=[jax.ShapeDtypeStruct(s, t) for s, t in out_shapes],
        scratch_shapes=scratch,
        cost_estimate=pl.CostEstimate(flops=flops, bytes_accessed=1, transcendentals=0),
        compiler_params=pltpu.CompilerParams(vmem_limit_bytes=mib * 2**20),
    )(*ins)


def run(pairs, sems, first=0):
    copies = [
        pltpu.make_async_copy(src, dst, sems.at[first + i]) for i, (src, dst) in enumerate(pairs)
    ]
    for copy in copies:
        copy.start()
    return copies


def cut_kernel(proj, part, sem):
    copy = pltpu.make_async_copy(proj.at[place(index("y"), BLOCK), :], part, sem)
    copy.start()
    copy.wait()


def cut(proj):
    return call(
        cut_kernel,
        (proj,),
        [((BLOCK, WIDTH), BF16)],
        [pltpu.SemaphoreType.DMA],
        4,
        out_specs=[VMEM],
    )[0]


def split_kernel(teacher, student, o1, o3, o2, sems):
    x, zh, c = (index(a) for a in ("x", "zh", "c"))
    pairs = []
    for s, out in ((1, o1), (3, o3), (2, o2)):
        pairs.append((student, out.at[pl.ds(TOK, TOK), :]))
        for j, (zh_at, c_at) in enumerate(pieces(zh, c)):
            pairs.append(
                (
                    teacher.at[:, columns((x + s) % N, zh_at, c_at)],
                    out.at[pl.ds(0, TOK), pl.ds(j * WIDTH, WIDTH)],
                )
            )
    for copy in run(pairs, sems):
        copy.wait()


def split(teacher, student):
    return call(
        split_kernel,
        (teacher, student),
        [((2 * TOK, 4 * WIDTH), BF16)] * 3,
        [pltpu.SemaphoreType.DMA((15,))],
        8,
        out_specs=[VMEM] * 3,
    )


def relay_kernel(p1, p3, lower, upper, sems):
    half = BLOCK // 2
    for copy in run([(p1.at[:half, :], lower), (p3.at[half:, :], upper)], sems):
        copy.wait()


def relay(*ins):
    return call(
        relay_kernel,
        ins,
        [((BLOCK // 2, WIDTH), BF16)] * 2,
        [pltpu.SemaphoreType.DMA((2,))],
        4,
        out_specs=[VMEM] * 2,
    )


def join_kernel(own, p1, p3, lower, upper, _, out, sems):
    y = index("y")
    half = BLOCK // 2

    def rows(s, first, size):
        return out.at[pl.ds(pl.multiple_of((y + N - s) % N * BLOCK + first, half), size), :]

    pairs = [
        (own, rows(0, 0, BLOCK)),
        (p1, rows(1, 0, BLOCK)),
        (p3, rows(3, 0, BLOCK)),
        (lower, rows(2, 0, half)),
        (upper, rows(2, half, half)),
    ]
    for copy in run(pairs, sems):
        copy.wait()


def join(parts):
    return call(
        join_kernel,
        parts,
        [((DS, WIDTH), BF16)],
        [pltpu.SemaphoreType.DMA((5,))],
        8,
        out_specs=[VMEM],
    )[0]


def mark_kernel(*refs):
    refs[-1][...] = jnp.zeros_like(refs[-1])


def mark(values, flops):
    return call(mark_kernel, values, [((8, 128), F32)], [], 1, flops, out_specs=[VMEM])[0]


def error_kernel(half, student, b1, b2, b3, w_own, w_other, teacher, errors, grads, *rest):
    students, targets, sems = rest
    x, zh, c = (index(a) for a in ("x", "zh", "c"))
    zh_at = zh if half == 0 else 1 - zh
    blocks = (b1, b2, b3)
    rows = [pl.ds(s * TOK, TOK) for s in range(N)]
    loads = run(
        [(student, students.at[rows[0], :])]
        + [(block.at[rows[1], :], students.at[row, :]) for block, row in zip(blocks, rows[1:])]
        + [
            (teacher.at[:, columns(x, zh_at, c_at)], targets.at[:, pl.ds(j * WIDTH, WIDTH)])
            for j, c_at in enumerate((c, 1 - c))
        ],
        sems,
    )
    for copy in loads:
        copy.wait()

    def one(j, weights):
        cols = pl.ds(j * WIDTH, WIDTH)
        away = pl.ds((half * 2 + j) * WIDTH, WIDTH)
        predicted = dot(students[...], weights[...], 1, 0)
        for s in range(N):
            target = targets[:, cols] if s == 0 else blocks[s - 1][rows[0], away]
            part = predicted[s * TOK : (s + 1) * TOK] - target.astype(F32)
            errors[rows[s], cols] = part.astype(BF16)

    one(1, w_other)
    turned = errors[:, pl.ds(WIDTH, WIDTH)].T

    def step(n, _):
        cols = place(n, BLOCK)
        grads[:, cols] = dot(turned, students[:, cols], 1, 0).astype(BF16)

    lax.fori_loop(0, N, step, None)
    one(0, w_own)


def error_and_other(half, student, blocks, w_own, w_other, teacher):
    n_tok = N * TOK
    return call(
        functools.partial(error_kernel, half),
        (student, *blocks, w_own, w_other, teacher),
        [((n_tok, 2 * WIDTH), BF16), ((WIDTH, DS), BF16)],
        [
            pltpu.VMEM((n_tok, DS), BF16),
            pltpu.VMEM((TOK, 2 * WIDTH), BF16),
            pltpu.SemaphoreType.DMA((6,)),
        ],
        12,
        BIG,
        in_specs=[ANY] + [VMEM] * 5 + [ANY],
        out_specs=[VMEM] * 2,
    )


def own_kernel(order, n_in, student, b1, b2, b3, error, there, *rest):
    ins, rest = rest[:n_in], rest[n_in:]
    *outs, students, sems = rest
    y = index("y")
    held = (student, *(block.at[pl.ds(TOK, TOK), :] for block in (b1, b2, b3)))
    spots = [place((y + s) % N, BLOCK) for s in order]
    loads = [
        run(
            [
                (ref.at[:, spot], students.at[k, pl.ds(s * TOK, TOK), :])
                for s, ref in enumerate(held)
            ],
            sems,
            4 * k,
        )
        for k, spot in enumerate(spots)
    ]
    turned = error[:, pl.ds(0, WIDTH)].T
    half = WIDTH // 2
    for k, s in enumerate(order):
        for copy in loads[k]:
            copy.wait()
        total = dot(turned, students[k], 1, 0) + there[:, spots[k]].astype(F32)
        low, high = total[:half], total[half:]
        if ins and s == 1:
            low = low + ins[0][...].astype(F32)
        elif ins and s == 3:
            high = high + ins[1][...].astype(F32)
        if s == 2:
            outs[0][...] = low.astype(BF16)
            outs[1][...] = high.astype(BF16)
        else:
            outs[k][:half] = low.astype(BF16)
            outs[k][half:] = high.astype(BF16)


def own_and_sum(order, students, error, there, ins=(), flops=1):
    n_tok, n = N * TOK, len(order)
    halves = [((WIDTH // 2, BLOCK), BF16)] * 2
    outs = halves if order == (2,) else [((WIDTH, BLOCK), BF16)] * 3
    return call(
        functools.partial(own_kernel, order, len(ins)),
        (*students, error, there, *ins),
        outs,
        [pltpu.VMEM((n, n_tok, BLOCK), BF16), pltpu.SemaphoreType.DMA((4 * n,))],
        10,
        flops,
        in_specs=[ANY] * 4 + [VMEM] * (2 + len(ins)),
        out_specs=[VMEM] * len(outs),
    )


def student_kernel(near, far, wa, wb, wc, wd, o0, o1, o3, low, high):
    errors, weights = (near, far), (wa, wb, wc, wd)

    def step(n, _):
        cols = place(n, BLOCK)
        total = None
        for p in range(4):
            term = dot(errors[p // 2][:, pl.ds(p % 2 * WIDTH, WIDTH)], weights[p][cols, :], 1, 1)
            total = term if total is None else total + term
        for s, out in ((0, o0), (1, o3), (3, o1)):
            out[:, cols] = total[s * TOK : (s + 1) * TOK].astype(BF16)
        low[:, cols] = total[2 * TOK : 2 * TOK + TOK // 2].astype(BF16)
        high[:, cols] = total[2 * TOK + TOK // 2 : 3 * TOK].astype(BF16)

    lax.fori_loop(0, N, step, None)


def student_part(near, far, weights):
    return call(
        student_kernel,
        (near, far, *weights),
        [((TOK, DS), BF16)] * 3 + [((TOK // 2, DS), BF16)] * 2,
        [],
        12,
        BIG,
        in_specs=[VMEM] * 6,
        out_specs=[VMEM] * 5,
    )


def pass_kernel(b1, b3, low, high, o1, o3):
    half = b1.shape[0] // 2
    o1[:half] = (b1[:half].astype(F32) + low[...].astype(F32)).astype(BF16)
    o1[half:] = b1[half:]
    o3[:half] = b3[:half]
    o3[half:] = (b3[half:].astype(F32) + high[...].astype(F32)).astype(BF16)


def y_kernel(a, b, c, own, other, out):
    zl = index("zl")

    def block(at):
        cols = place(at, ROWS)
        return a[:, cols].astype(F32) + b[:, cols].astype(F32) + c[:, cols].astype(F32)

    own[...] = block(zl)
    other[...] = block(zl ^ 2)
    out[:, :ROWS] = block(zl ^ 1).astype(BF16)
    out[:, ROWS:] = block(zl ^ 3).astype(BF16)


def pair_kernel(own, other, got, total, out):
    total[...] = own[...] + got[:, :ROWS].astype(F32)
    out[...] = (other[...] + got[:, ROWS:].astype(F32)).astype(BF16)


def z_kernel(own, got, out):
    out[...] = (own[...] + got[...].astype(F32)).astype(BF16)


def final_kernel(own, got, far, out):
    total = own[...] + got[...].astype(F32) + far[...].astype(F32)
    out[...] = total.T * (1.0 / math.sqrt(TOK * 256))


def student_sum_kernel(own, p1, p3, out):
    total = own[...].astype(F32) + p1[...].astype(F32)
    out[...] = (total + p3[...].astype(F32)).astype(BF16)


def in_vmem(kernel, ins, outs, flops=1):
    return call(kernel, ins, outs, [], 8, flops, in_specs=[VMEM] * len(ins), out_specs=[VMEM] * len(outs))


def over(axis, blocks, *done):
    got = {s: shift(after(b, *done), axis, s) for s, b in zip((1, 3, 2), blocks)}
    return [got[s] for s in (1, 2, 3)]


def body(teacher, student, proj):
    blocks = over("x", split(teacher, student))
    students = (student, *blocks)
    proj_b = shift(proj, "c", 1)
    part = after(shift(cut(proj), "zh", 1), proj_b)

    p1, p3 = shift(part, "y", 1), shift(part, "y", 3)
    lower, upper = relay(p1, p3)
    lower, upper = shift(lower, "y", 1), shift(upper, "y", 3)
    proj_c = join([part, p1, p3, lower, upper, mark(blocks, SMALL)])
    proj_d = shift(proj_c, "c", 1)

    near, there = error_and_other(0, student, blocks, after(proj, proj_c), proj_b, teacher)
    near_there = shift(there, "c", 1)
    far, there = error_and_other(1, student, blocks, after(proj_c, near), proj_d, teacher)
    far_there = shift(there, "c", 1)

    sent = own_and_sum((2,), students, near, after(near_there, far))
    near_in = [shift(sent[0], "y", 1), shift(sent[1], "y", 3)]
    sent = own_and_sum((2,), students, far, after(far_there, *sent))
    far_in = [shift(sent[0], "y", 1), shift(sent[1], "y", 3)]
    far_sum = own_and_sum((1, 3, 0), students, far, after(far_there, *sent))
    weights = (proj, proj_b, proj_c, after(proj_d, *far_sum))
    partial = student_part(near, far, weights)
    terms = [*far_sum[:2], after(far_in[0], partial[0], *near_in), far_in[1]]
    ready = in_vmem(pass_kernel, terms, [((WIDTH, BLOCK), BF16)] * 2)
    passed = shift(partial[3], "x", 1), shift(partial[4], "x", 3)
    back = in_vmem(pass_kernel, [*partial[1:3], *passed], [((TOK, DS), BF16)] * 2, BIG)
    back = shift(after(back[0], ready[0]), "x", 1), shift(after(back[1], ready[0]), "x", 3)
    far_y = [far_sum[2], shift(ready[0], "y", 1), shift(ready[1], "y", 3)]
    near_sum = own_and_sum(
        (1, 3, 0), students, near, after(near_there, *ready), near_in
    )
    sent = [after(b, *far_y[1:]) for b in near_sum[:2]]
    near_y = [near_sum[2], shift(sent[0], "y", 1), shift(sent[1], "y", 3)]

    def over_y_and_pair(terms, flops):
        outs = [((WIDTH, ROWS), F32)] * 2 + [((WIDTH, 2 * ROWS), BF16)]
        own, other, out = in_vmem(y_kernel, terms, outs, flops)
        outs = [((WIDTH, ROWS), F32), ((WIDTH, ROWS), BF16)]
        own, out = in_vmem(pair_kernel, [own, other, swap(out, 1)], outs)
        return [own, swap(out, 2)]

    far_terms = over_y_and_pair(far_y, 1)
    far_terms = [after(far_terms[0], *back), far_terms[1]]
    far_part = in_vmem(z_kernel, far_terms, [((WIDTH, ROWS), BF16)], MEDIUM)[0]
    near_terms = over_y_and_pair(near_y, BIG)
    far_part = shift(far_part, "zh", 1)
    grad_student = in_vmem(
        student_sum_kernel, [partial[0], *back], [((TOK, DS), BF16)]
    )[0]
    grad_proj = in_vmem(final_kernel, [*near_terms, far_part], [((ROWS, WIDTH), F32)])[0]
    return grad_proj, grad_student


def solution(mesh):
    fine = Mesh(mesh.devices.reshape(4, 4, 4, 2, 2), ALL)
    tokens = P(ALL, None)
    return jax.shard_map(
        body,
        mesh=fine,
        in_specs=(tokens, tokens, P(None, ("x", "zh", "c"))),
        out_specs=(P(("y", "zl"), ("x", "zh", "c")), tokens),
        check_vma=False,
    )
```
